32 devices in a mesh: pool: 4 (over z), ctx: 8 (over y, x, core).
Axes of the slice: x: 2, y: 2, z: 4, core: 2. Of those that a mesh axis runs over, the one named last changes fastest.
Arguments:
- question_q: bfloat16 [2048, 4096], P('ctx', 'pool'), may hold values from -6 to 6
- question_kv: bfloat16 [2, 2048, 512], P(None, 'ctx', 'pool'), may hold values from -6 to 6
- cache_kv: bfloat16 [64, 2, 64, 512], P(('pool', 'ctx')), may hold values from -6 to 6
- placement: int32 [32], P('ctx'), may hold values from -1 to 63, as said below
- offsets: int32 [32], P('ctx'), may hold values from 0 to 1984
Outputs:
- attended: bfloat16 [2048, 4096], P('ctx', 'pool')
The draws below stay inside these ranges and needn't reach their ends.
Inputs may be any that keep to these rules, and one draw needn't show every extreme that they name: `placement`: owner o's slots are entries o * 4 to o * 4 + 3; the live ones come first, every owner has at least one and some owner has all 4; no pool block is placed twice. Of the blocks held by the devices of one index c of ctx (ids b with (b // 2) % 8 == c), at most 4 are placed, and exactly 4 for some index.
All inputs are finite; a program needn't handle non-finite values.
Results may differ from the reference program's by a relative error of at most 0.012.
Values may be sent and summed in bfloat16 or wider, within the bound.
A program may use at most 64 MiB of HBM per device.

```python
import math
import jax
import jax.numpy as jnp
from jax import lax

H = 32
KEY_VALUE_HEADS = 4
HEAD_SIZE = 128
PASSAGE_TOKENS = 64
OWNER_SLOTS = 4
HOLD = 2
QLEN = 2048
REQUEST_SLOTS = 32
POOLB = 64
QUESTION_START = 2048


def planted_rows(key):
    key_pick, key_sign = jax.random.split(key)
    planted_count = 8
    candidates = QLEN // 4
    picks = jax.random.permutation(key_pick, candidates)[:planted_count]
    tokens = (4 * picks + 2).astype(jnp.int32)
    levels = 2.5 + 0.5 * jnp.arange(planted_count, dtype=jnp.float32)
    signs = jnp.where(jax.random.bernoulli(key_sign, 0.5, (planted_count, KEY_VALUE_HEADS, HEAD_SIZE)), 1.0, -1.0).astype(jnp.float32)
    return (tokens, levels, signs)


def draw_question_q(key, part):
    tokens, levels, signs = planted_rows(key)
    key = jax.random.fold_in(key, 21)
    shape = (QLEN, H * HEAD_SIZE)
    base_field = jnp.clip(jax.random.normal(key, shape, jnp.float32), -6.0, 6.0)
    group_size = H // KEY_VALUE_HEADS
    head_signs = jnp.repeat(signs, group_size, axis=1).reshape(tokens.shape[0], H * HEAD_SIZE) * levels[:, None]
    row_index = jnp.arange(QLEN, dtype=jnp.int32)[:, None]
    for planted in range(tokens.shape[0]):
        base_field = jnp.where(row_index == tokens[planted], head_signs[planted][None, :], base_field)
    return base_field.astype(jnp.bfloat16)


def draw_question_kv(key, part):
    tokens, levels, signs = planted_rows(key)
    key = jax.random.fold_in(key, 23)
    shape = (2, QLEN, KEY_VALUE_HEADS * HEAD_SIZE)
    base_field = jnp.clip(jax.random.normal(key, shape, jnp.float32), -6.0, 6.0)
    half_width = HEAD_SIZE // 2
    frequency = 500000.0 ** (-jnp.arange(half_width, dtype=jnp.float32) / half_width)
    cosine = jnp.cos(frequency)
    sine_part = jnp.sin(frequency)
    spread = 2.0 / (levels * math.sqrt(HEAD_SIZE))
    lesser = (4.0 - spread)[:, None, None] * signs
    first_half = lesser[..., :half_width]
    second_half = lesser[..., half_width:]
    second_keys = jnp.concatenate([first_half * cosine - second_half * sine_part, second_half * cosine + first_half * sine_part], axis=-1)
    row_index = jnp.arange(QLEN, dtype=jnp.int32)[:, None]
    keys_now = base_field[0]
    for planted in range(tokens.shape[0]):
        keys_now = jnp.where(row_index == tokens[planted], (4.0 * signs[planted]).reshape(1, KEY_VALUE_HEADS * HEAD_SIZE), keys_now)
        keys_now = jnp.where(row_index == tokens[planted] - 1, second_keys[planted].reshape(1, KEY_VALUE_HEADS * HEAD_SIZE), keys_now)
    return jnp.stack([keys_now, base_field[1]], axis=0).astype(jnp.bfloat16)


def draw_placement(key, part):
    key = jax.random.fold_in(key, 11)
    key_count, key_full, key_order, key_column, key_local = jax.random.split(key, 5)
    context_owners = REQUEST_SLOTS // OWNER_SLOTS
    counts = jax.random.randint(key_count, (context_owners,), 1, OWNER_SLOTS + 1)
    fullest = jax.random.randint(key_full, (), 0, context_owners)
    counts = jnp.where(jnp.arange(context_owners) == fullest, OWNER_SLOTS, counts)
    slot_index = jnp.arange(OWNER_SLOTS)[None, :]
    is_live = (slot_index < counts[:, None]).reshape(-1)
    live_rank = jnp.cumsum(is_live.astype(jnp.int32)) - 1
    entries = context_owners * OWNER_SLOTS
    entry_index = jnp.arange(entries, dtype=jnp.int32)
    chosen_column = jax.random.randint(key_column, (), 0, context_owners)
    entry_scores = jnp.where(entry_index % context_owners == chosen_column, 0, entries) + jax.random.permutation(key_order, entries)
    entry_order = jnp.argsort(entry_scores)
    entry = entry_order[jnp.clip(live_rank, 0, entries - 1)]
    column = entry % context_owners
    copy_index = entry // context_owners
    local_count = POOLB // context_owners
    local_bits = jax.random.randint(key_local, (context_owners, local_count), 0, 1 << 20)
    local_order = jnp.argsort(local_bits * local_count + jnp.arange(local_count)[None, :], axis=1)
    local_index = local_order[column, copy_index]
    pool_index = local_index // HOLD
    held_index = local_index % HOLD
    block_ids = (pool_index * context_owners + column) * HOLD + held_index
    return jnp.where(is_live, block_ids, -1).astype(jnp.int32)


def with_ends(drawn, rng, smallest, largest):
    extent = drawn.shape
    index_at = [jax.random.randint(jax.random.fold_in(rng, axis), (), 0, extent[axis]) for axis in range(len(extent))]
    drawn = drawn.at[tuple(index_at)].set(smallest)
    longest = extent.index(max(extent))
    index_at[longest] = (index_at[longest] + 1) % extent[longest]
    return drawn.at[tuple(index_at)].set(largest)


def shard_levels(own_key, shape, shards, smallest, largest):
    level, own = 1.0, jax.random.fold_in(own_key, 6)
    for position, parts in shards:
        heights = jnp.exp(jax.random.uniform(jax.random.fold_in(own, position), (parts,), jnp.float32, smallest / len(shards), largest / len(shards)))
        level = level * jnp.repeat(heights, shape[position] // parts).reshape([-1 if axis == position else 1 for axis in range(len(shape))])
    return level


def scatter_about(key, dims, scale, limit, cuts=(), held_as=jnp.bfloat16):
    values = jax.random.normal(key, dims, jnp.float32) * scale
    if len(cuts) > 0:
        values = shard_levels(key, dims, cuts, -0.22, 0.18) * values
    return jnp.clip(values, min=-limit, max=limit).astype(held_as)


def setup_inputs(seed: int = 0) -> dict:
    seeds = jax.random.split(jax.random.key(seed), 6)
    return {
        "question_q": draw_question_q(jax.random.fold_in(seeds[5], 71), 0),
        "question_kv": draw_question_kv(jax.random.fold_in(seeds[5], 71), 0),
        "cache_kv": scatter_about(seeds[2], (POOLB, 2, PASSAGE_TOKENS, KEY_VALUE_HEADS * HEAD_SIZE), 1.0, 6.0, ((0, 32),)),
        "placement": draw_placement(jax.random.fold_in(seeds[5], 71), 0),
        "offsets": with_ends(jax.random.randint(seeds[4], (REQUEST_SLOTS,), 0, QUESTION_START - PASSAGE_TOKENS + 1), jax.random.fold_in(seeds[4], 1), 0, QUESTION_START - PASSAGE_TOKENS).astype(jnp.int32),
    }


rope_base = 500000.0
masked_score = -1.0e30


def rope_tables(positions, half_width):
    frequency = rope_base ** (-jnp.arange(half_width, dtype=jnp.float32) / half_width)
    angles = positions.astype(jnp.float32)[:, None] * frequency[None, :]
    return jnp.cos(angles), jnp.sin(angles)


def rotate(vectors, cosine, sine_part):
    half_width = vectors.shape[-1] // 2
    first_half = vectors[..., :half_width]
    second_half = vectors[..., half_width:]
    return jnp.concatenate([first_half * cosine - second_half * sine_part, second_half * cosine + first_half * sine_part], axis=-1)


def reference(question_q, question_kv, cache_kv, placement, offsets):
    half_width = HEAD_SIZE // 2
    group_size = H // KEY_VALUE_HEADS
    score_scale = HEAD_SIZE ** -0.5
    is_live = placement >= 0
    safe_ids = jnp.maximum(placement, 0).astype(jnp.int32)
    passage_blocks = cache_kv[safe_ids]
    key_offsets = jnp.repeat(offsets, PASSAGE_TOKENS)
    key_live = jnp.repeat(is_live, PASSAGE_TOKENS)
    cosine, sine_part = rope_tables(key_offsets, half_width)
    cached_passage_keys = passage_blocks[:, 0].reshape(REQUEST_SLOTS * PASSAGE_TOKENS, KEY_VALUE_HEADS, HEAD_SIZE).transpose(1, 0, 2).astype(jnp.float32)
    cached_passage_keys = rotate(cached_passage_keys, cosine, sine_part).astype(jnp.bfloat16)
    cached_passage_values = passage_blocks[:, 1].reshape(REQUEST_SLOTS * PASSAGE_TOKENS, KEY_VALUE_HEADS, HEAD_SIZE).transpose(1, 0, 2)
    query_pos = QUESTION_START + jnp.arange(QLEN, dtype=jnp.int32)
    cos_query, sin_query = rope_tables(query_pos, half_width)
    raw_queries = question_q.reshape(QLEN, H, HEAD_SIZE).transpose(1, 0, 2).astype(jnp.float32)
    queries = rotate(raw_queries, cos_query, sin_query).astype(jnp.bfloat16)
    raw_own = question_kv[0].reshape(QLEN, KEY_VALUE_HEADS, HEAD_SIZE).transpose(1, 0, 2).astype(jnp.float32)
    own_keys = rotate(raw_own, cos_query, sin_query).astype(jnp.bfloat16)
    own_values = question_kv[1].reshape(QLEN, KEY_VALUE_HEADS, HEAD_SIZE).transpose(1, 0, 2)
    block_rows = math.gcd(QLEN, 1024)
    key_index = jnp.arange(QLEN, dtype=jnp.int32)

    def one_head(head):
        kv_index = head // group_size
        query_rows = queries[head].astype(jnp.float32)
        keys_passage = cached_passage_keys[kv_index].astype(jnp.float32)
        values_passage = cached_passage_values[kv_index].astype(jnp.float32)
        keys_own = own_keys[kv_index].astype(jnp.float32)
        values_own = own_values[kv_index].astype(jnp.float32)

        def one_block(block_index):
            rows_here = lax.dynamic_slice_in_dim(query_rows, block_index * block_rows, block_rows, 0)
            query_index = block_index * block_rows + jnp.arange(block_rows, dtype=jnp.int32)
            scores_passage = jnp.einsum("qd,kd->qk", rows_here, keys_passage) * score_scale
            scores_passage = jnp.where(key_live[None, :], scores_passage, masked_score)
            causal = key_index[None, :] <= query_index[:, None]
            scores_own = jnp.einsum("qd,kd->qk", rows_here, keys_own) * score_scale
            scores_own = jnp.where(causal, scores_own, masked_score)
            row_max = jnp.maximum(jnp.max(scores_passage, axis=1), jnp.max(scores_own, axis=1))
            weights_passage = jnp.where(key_live[None, :], jnp.exp(scores_passage - row_max[:, None]), 0.0)
            weights_own = jnp.where(causal, jnp.exp(scores_own - row_max[:, None]), 0.0)
            totals = jnp.sum(weights_passage, axis=1) + jnp.sum(weights_own, axis=1)
            rounded_passage = lax.optimization_barrier(weights_passage.astype(jnp.bfloat16)).astype(jnp.float32)
            rounded_own = lax.optimization_barrier(weights_own.astype(jnp.bfloat16)).astype(jnp.float32)
            numerator = jnp.einsum("qk,kd->qd", rounded_passage, values_passage) + jnp.einsum("qk,kd->qd", rounded_own, values_own)
            return numerator / totals[:, None]

        return lax.map(one_block, jnp.arange(QLEN // block_rows, dtype=jnp.int32))

    result = lax.map(one_head, jnp.arange(H, dtype=jnp.int32))
    result = result.reshape(H, QLEN, HEAD_SIZE).transpose(1, 0, 2).reshape(QLEN, H * HEAD_SIZE)
    return result.astype(jnp.bfloat16)
```

```python
import functools
import math

import jax
import jax.numpy as jnp
import numpy as np
from jax import lax
from jax.experimental import pallas as pl
from jax.experimental.pallas import tpu as pltpu
from jax.sharding import PartitionSpec as P

HEAD = 128
HALF = HEAD // 2
ROPE_BASE = 500000.0
MASKED = -1e30
LOG2_SCALE = HEAD**-0.5 * math.log2(math.e)
MESH = pl.DeviceIdType.MESH


def frequency_rows():
    frequency = ROPE_BASE ** (-np.arange(HALF, dtype=np.float64) / HALF)
    return np.tile(np.concatenate([frequency, frequency]).astype(np.float32)[None, :], (8, 1))


def flip_chip(chip, step, chips):
    result, bit = 0, 1
    while bit < chips:
        a = (chip // bit) % 2
        b = (step // bit) % 2
        result = result + bit * (a + b - 2 * a * b)
        bit *= 2
    return result


def signed(sine):
    lane = lax.broadcasted_iota(jnp.int32, sine.shape, 1)
    return jnp.where(lane < HALF, -sine, sine)


def turn(vectors, cosine, sine_signed):
    return vectors * cosine + pltpu.roll(vectors, HALF, 1) * sine_signed


def kernel(
    counts,
    q_hbm,
    kv_hbm,
    cache_hbm,
    place_ref,
    offset_ref,
    freq_ref,
    out_ref,
    q_raw,
    q_rot,
    kv_raw,
    own,
    pas,
    held,
    meta,
    k_now,
    v_now,
    top,
    acc,
    local_sem,
    pool_send,
    pool_recv,
    meta_send,
    meta_recv,
    own_send,
    own_recv,
    own_fwd_send,
    own_fwd_recv,
    pas_send,
    pas_recv,
    pas_fwd_send,
    pas_fwd_recv,
):
    pools, ctxs = counts
    chips = ctxs // 2
    p = lax.axis_index("pool")
    c = lax.axis_index("ctx")
    t = c // 2
    core = c % 2
    sibling = 2 * t + 1 - core
    rows = q_raw.shape[0]
    heads = q_rot.shape[0]
    hold = held.shape[1]
    block = held.shape[3]
    slots = place_ref.shape[0]
    shard = slots * block
    question_start = ctxs * slots * block

    load_q = pltpu.make_async_copy(q_hbm, q_raw, local_sem.at[0])
    load_kv = pltpu.make_async_copy(kv_hbm, kv_raw, local_sem.at[1])
    load_held = pltpu.make_async_copy(
        cache_hbm.at[:, :, :, pl.ds(pl.multiple_of(p * HEAD, HEAD), HEAD)],
        held.at[p],
        local_sem.at[2],
    )
    load_kv.start()
    load_held.start()
    load_q.start()

    barrier = pltpu.get_barrier_semaphore()
    for d in range(1, pools):
        pl.semaphore_signal(barrier, inc=1, device_id=((p + d) % pools, c), device_id_type=MESH)

    def greet(d, _):
        pl.semaphore_signal(barrier, inc=1, device_id=(p, (c + d) % ctxs), device_id_type=MESH)
        return 0

    lax.fori_loop(1, ctxs, greet, 0)

    row8 = lax.broadcasted_iota(jnp.int32, (8, HEAD), 0)
    place_tile = jnp.full((8, HEAD), -1, jnp.int32)
    offset_tile = jnp.zeros((8, HEAD), jnp.int32)
    for i in range(slots):
        place_tile = jnp.where(row8 == i, place_ref[i], place_tile)
        offset_tile = jnp.where(row8 == i, offset_ref[i], offset_tile)
    meta[c, 0] = place_tile
    meta[c, 1] = offset_tile

    freq = freq_ref[0:1, :]
    token = lax.broadcasted_iota(jnp.int32, (rows, HEAD), 0) + (question_start + c * rows)
    angle = token.astype(jnp.float32) * freq
    cos_q = jnp.cos(angle)
    sin_q = signed(jnp.sin(angle))

    load_kv.wait()
    own[c, 0] = turn(kv_raw[0].astype(jnp.float32), cos_q, sin_q).astype(jnp.bfloat16)
    own[c, 1] = kv_raw[1]

    pl.semaphore_wait(barrier, pools - 1 + ctxs - 1)

    def pool_copy(d):
        target = (p + d) % pools
        return pltpu.make_async_remote_copy(
            src_ref=cache_hbm.at[:, :, :, pl.ds(pl.multiple_of(target * HEAD, HEAD), HEAD)],
            dst_ref=held.at[p],
            send_sem=pool_send.at[d],
            recv_sem=pool_recv.at[d],
            device_id=(target, c),
            device_id_type=MESH,
        )

    def meta_copy(d):
        return pltpu.make_async_remote_copy(
            src_ref=meta.at[c],
            dst_ref=meta.at[c],
            send_sem=meta_send.at[d],
            recv_sem=meta_recv.at[d],
            device_id=(p, (c + d) % ctxs),
            device_id_type=MESH,
        )

    def chip_copy(buffer, send, recv, d):
        return pltpu.make_async_remote_copy(
            src_ref=buffer.at[c],
            dst_ref=buffer.at[c],
            send_sem=send.at[d],
            recv_sem=recv.at[d],
            device_id=(p, 2 * flip_chip(t, d, chips) + core),
            device_id_type=MESH,
        )

    def forward_copy(buffer, send, recv, d):
        place = 2 * flip_chip(t, d, chips) + core
        return pltpu.make_async_remote_copy(
            src_ref=buffer.at[place],
            dst_ref=buffer.at[place],
            send_sem=send.at[d],
            recv_sem=recv.at[d],
            device_id=(p, sibling),
            device_id_type=MESH,
        )

    own_sems = (own, own_send, own_recv)
    own_fwd = (own, own_fwd_send, own_fwd_recv)
    pas_sems = (pas, pas_send, pas_recv)
    pas_fwd = (pas, pas_fwd_send, pas_fwd_recv)

    for d in range(1, pools):
        pool_copy(d).start()
    forward_copy(*own_fwd, 0).start()

    def start_meta(d, _):
        meta_copy(d).start()
        return 0

    lax.fori_loop(1, ctxs, start_meta, 0)

    def start_own(d, _):
        @pl.when(flip_chip(t, d, chips) > t)
        def _():
            chip_copy(*own_sems, d).start()

        return 0

    lax.fori_loop(1, chips, start_own, 0)

    load_q.wait()
    for g in range(heads):
        vectors = q_raw[:, g * HEAD : (g + 1) * HEAD].astype(jnp.float32)
        q_rot[g] = turn(vectors, cos_q, sin_q).astype(jnp.bfloat16)

    ones = jnp.ones((2 * shard, HEAD), jnp.bfloat16)

    def attend(keys, first, allowed):
        width = keys.shape[0]
        wide = width // HEAD

        def one_head(g, _):
            scores = lax.dot_general(
                q_rot[g], keys[...], (((1,), (1,)), ((), ())), preferred_element_type=jnp.float32
            )
            if allowed is not None:
                scores = jnp.where(allowed(scores.shape), scores, MASKED)
            peak = jnp.broadcast_to(jnp.max(scores, axis=1, keepdims=True), (rows, HEAD))
            if not first:
                before = top[g]
                peak = jnp.maximum(before, peak)
            weights = jnp.exp2((scores - jnp.concatenate([peak] * wide, axis=1)) * LOG2_SCALE)
            product = jnp.dot(
                weights.astype(jnp.bfloat16), v_now[...], preferred_element_type=jnp.float32
            )
            if first:
                acc[g] = product
            else:
                shrink = jnp.exp2((before - peak) * LOG2_SCALE)
                acc[g] = acc[g] * jnp.concatenate([shrink, shrink], axis=1) + product
            top[g] = peak
            return 0

        lax.fori_loop(0, heads, one_head, 0)

    def gather_chunk(buffer, chip):
        k_now[...] = buffer[pl.ds(2 * chip, 2), 0].reshape(2 * shard, HEAD)
        v_now[:, :HEAD] = buffer[pl.ds(2 * chip, 2), 1].reshape(2 * shard, HEAD)

    forward_copy(*own_fwd, 0).wait_recv()
    gather_chunk(own, t)
    v_now[:, HEAD:] = ones

    def causal(shape):
        key = lax.broadcasted_iota(jnp.int32, shape, 1)
        query = lax.broadcasted_iota(jnp.int32, shape, 0) + core * rows
        return key <= query

    attend(k_now, True, causal)

    def own_step(d, _):
        source = flip_chip(t, d, chips)

        @pl.when(source < t)
        def _():
            chip_copy(*own_sems, d).wait_recv()
            forward_copy(*own_fwd, d).start()
            forward_copy(*own_fwd, d).wait_recv()
            gather_chunk(own, source)
            attend(k_now, False, None)

        return 0

    lax.fori_loop(1, 2, own_step, 0)

    def wait_meta(d, _):
        meta_copy(d).wait_recv()
        return 0

    lax.fori_loop(1, ctxs, wait_meta, 0)
    load_held.wait()
    for d in range(1, pools):
        pool_copy(d).wait_recv()

    places = meta[:, 0]
    offsets = meta[:, 1].astype(jnp.float32)
    live, where_to, rank = [], [], []
    filled = jnp.zeros((1, HEAD), jnp.float32)
    for b in range(pools * hold):
        block_id = ((b // hold) * ctxs + c) * hold + b % hold
        match = jnp.where(places == block_id, 1.0, 0.0)
        live.append(jnp.sum(jnp.sum(match, axis=0), axis=0, keepdims=True))
        where_to.append(jnp.sum(jnp.sum(match * offsets, axis=0), axis=0, keepdims=True))
        rank.append(filled)
        filled = filled + live[-1]
    for k in range(slots):
        key_sum = jnp.zeros((block, HEAD), jnp.float32)
        value_sum = jnp.zeros((block, HEAD), jnp.float32)
        offset = jnp.zeros((1, HEAD), jnp.float32)
        for b in range(pools * hold):
            pick = jnp.where(rank[b] == float(k), live[b], 0.0)
            key_sum = key_sum + pick * held[b // hold, b % hold, 0].astype(jnp.float32)
            value_sum = value_sum + pick * held[b // hold, b % hold, 1].astype(jnp.float32)
            offset = offset + pick * where_to[b]
        angle = jnp.broadcast_to(offset * freq, (8, HEAD))
        cos_k = jnp.cos(angle)[0:1]
        sin_k = signed(jnp.sin(angle))[0:1]
        pas[c, 0, k * block : (k + 1) * block] = turn(key_sum, cos_k, sin_k).astype(jnp.bfloat16)
        pas[c, 1, k * block : (k + 1) * block] = value_sum.astype(jnp.bfloat16)

    forward_copy(*pas_fwd, 0).start()

    def start_pas(d, _):
        chip_copy(*pas_sems, d).start()
        return 0

    lax.fori_loop(1, chips, start_pas, 0)

    lax.fori_loop(2, chips, own_step, 0)

    hold_bits = hold.bit_length() - 1

    def pas_step(d, _):
        source = flip_chip(t, d, chips)

        @pl.when(d > 0)
        def _():
            chip_copy(*pas_sems, d).wait_recv()
            forward_copy(*pas_fwd, d).start()

        forward_copy(*pas_fwd, d).wait_recv()
        v_now[:, :HEAD] = pas[pl.ds(2 * source, 2), 1].reshape(2 * shard, HEAD)
        seen = own[c, 0, 0:16].astype(jnp.float32)[0:1]
        all_places = meta[:, 0]
        holder = lax.shift_right_logical(all_places, hold_bits) & (ctxs - 1)
        for side in range(2):
            column = 2 * source + side
            mine = jnp.where((all_places >= 0) & (holder == column), 1.0, 0.0)
            count = jnp.sum(jnp.sum(mine, axis=0), axis=0, keepdims=True)
            for k in range(slots):
                flag = jnp.broadcast_to(jnp.where(count > float(k), 1.0, 0.0), (block, HEAD))
                at = side * shard + k * block
                keys = pas[column, 0, k * block : (k + 1) * block].astype(jnp.float32)
                k_now[at : at + block] = jnp.where(flag > 0.0, keys, seen).astype(jnp.bfloat16)
                v_now[at : at + block, HEAD:] = flag.astype(jnp.bfloat16)
        attend(k_now, False, None)
        return 0

    lax.fori_loop(0, chips, pas_step, 0)

    for g in range(heads):
        out_ref[:, g * HEAD : (g + 1) * HEAD] = (
            acc[g, :, :HEAD] / acc[g, :, HEAD:]
        ).astype(jnp.bfloat16)

    for d in range(1, pools):
        pool_copy(d).wait_send()

    def end_meta(d, _):
        meta_copy(d).wait_send()
        return 0

    lax.fori_loop(1, ctxs, end_meta, 0)
    forward_copy(*own_fwd, 0).wait_send()
    forward_copy(*pas_fwd, 0).wait_send()

    def end_chips(d, _):
        other = flip_chip(t, d, chips)

        @pl.when(other > t)
        def _():
            chip_copy(*own_sems, d).wait_send()

        @pl.when(other < t)
        def _():
            forward_copy(*own_fwd, d).wait_send()

        chip_copy(*pas_sems, d).wait_send()
        forward_copy(*pas_fwd, d).wait_send()
        return 0

    lax.fori_loop(1, chips, end_chips, 0)


def shards(counts, question_q, question_kv, cache_kv, placement, offsets):
    pools, ctxs = counts
    chips = ctxs // 2
    rows, width = question_q.shape
    heads = width // HEAD
    hold, _, block, _ = cache_kv.shape
    slots = placement.shape[0]
    shard = slots * block
    dma = pltpu.SemaphoreType.DMA
    any_space = pl.BlockSpec(memory_space=pl.ANY)
    return pl.pallas_call(
        functools.partial(kernel, counts),
        out_shape=jax.ShapeDtypeStruct((rows, width), jnp.bfloat16),
        in_specs=[
            any_space,
            any_space,
            any_space,
            pl.BlockSpec(memory_space=pltpu.SMEM),
            pl.BlockSpec(memory_space=pltpu.SMEM),
            pl.BlockSpec(memory_space=pltpu.VMEM),
        ],
        out_specs=pl.BlockSpec(memory_space=pltpu.VMEM),
        scratch_shapes=[
            pltpu.VMEM((rows, width), jnp.bfloat16),
            pltpu.VMEM((heads, rows, HEAD), jnp.bfloat16),
            pltpu.VMEM((2, rows, HEAD), jnp.bfloat16),
            pltpu.VMEM((ctxs, 2, rows, HEAD), jnp.bfloat16),
            pltpu.VMEM((ctxs, 2, shard, HEAD), jnp.bfloat16),
            pltpu.VMEM((pools, hold, 2, block, HEAD), jnp.bfloat16),
            pltpu.VMEM((ctxs, 2, 8, HEAD), jnp.int32),
            pltpu.VMEM((2 * shard, HEAD), jnp.bfloat16),
            pltpu.VMEM((2 * shard, 2 * HEAD), jnp.bfloat16),
            pltpu.VMEM((heads, rows, HEAD), jnp.float32),
            pltpu.VMEM((heads, rows, 2 * HEAD), jnp.float32),
            dma((3,)),
            dma((pools,)),
            dma((pools,)),
            dma((ctxs,)),
            dma((ctxs,)),
            dma((chips,)),
            dma((chips,)),
            dma((chips,)),
            dma((chips,)),
            dma((chips,)),
            dma((chips,)),
            dma((chips,)),
            dma((chips,)),
        ],
        compiler_params=pltpu.CompilerParams(
            collective_id=0, has_side_effects=True, vmem_limit_bytes=40 * 1024 * 1024
        ),
        name="attend_question",
    )(question_q, question_kv, cache_kv, placement, offsets, jnp.asarray(frequency_rows()))


def solution(mesh):
    counts = (mesh.shape["pool"], mesh.shape["ctx"])
    in_specs = (
        P("ctx", "pool"),
        P(None, "ctx", "pool"),
        P(("pool", "ctx"), None, None, None),
        P("ctx"),
        P("ctx"),
    )
    return jax.shard_map(
        functools.partial(shards, counts),
        mesh=mesh,
        in_specs=in_specs,
        out_specs=P("ctx", "pool"),
        check_vma=False,
    )
```

```python
import functools
import math

import jax
import jax.numpy as jnp
import numpy as np
from jax import lax
from jax.experimental import pallas as pl
from jax.experimental.pallas import tpu as pltpu
from jax.sharding import PartitionSpec as P

HEAD = 128
HALF = HEAD // 2
ROPE_BASE = 500000.0
MASKED = -1e30
LOG2_SCALE = HEAD**-0.5 * math.log2(math.e)
MESH = pl.DeviceIdType.MESH


def angle_tables(rows):
    frequency = ROPE_BASE ** (-np.arange(HALF, dtype=np.float64) / HALF)
    frequency = np.concatenate([frequency, frequency])
    angles = np.arange(rows)[:, None] * frequency[None, :]
    parts = [np.cos(angles), np.sin(angles), np.tile(frequency[None, :], (8, 1))]
    return np.concatenate(parts).astype(np.float32)


def flip_chip(chip, step, chips):
    result, bit = 0, 1
    while bit < chips:
        a = (chip // bit) % 2
        b = (step // bit) % 2
        result = result + bit * (a + b - 2 * a * b)
        bit *= 2
    return result


def signed(sine):
    lane = lax.broadcasted_iota(jnp.int32, sine.shape, 1)
    return jnp.where(lane < HALF, -sine, sine)


def turn(vectors, cosine, sine_signed):
    return vectors * cosine + pltpu.roll(vectors, HALF, 1) * sine_signed


def kernel(
    counts,
    q_hbm,
    kv_hbm,
    cache_hbm,
    place_hbm,
    offset_hbm,
    table_hbm,
    out_ref,
    place_ref,
    offset_ref,
    table_ref,
    q_raw,
    q_rot,
    kv_raw,
    own,
    pas,
    held,
    meta,
    k_now,
    v_now,
    top,
    acc,
    local_sem,
    pool_send,
    pool_recv,
    meta_send,
    meta_recv,
    own_send,
    own_recv,
    own_fwd_send,
    own_fwd_recv,
    pas_send,
    pas_recv,
    pas_fwd_send,
    pas_fwd_recv,
):
    pools, ctxs = counts
    chips = ctxs // 2
    p = lax.axis_index("pool")
    c = lax.axis_index("ctx")
    t = c // 2
    core = c % 2
    sibling = 2 * t + 1 - core
    rows = q_raw.shape[0]
    heads = q_rot.shape[0]
    hold = held.shape[1]
    block = held.shape[3]
    slots = place_ref.shape[0]
    shard = slots * block
    question_start = ctxs * slots * block

    load_q = pltpu.make_async_copy(q_hbm, q_raw, local_sem.at[0])
    load_kv = pltpu.make_async_copy(kv_hbm, kv_raw, local_sem.at[1])
    load_held = pltpu.make_async_copy(
        cache_hbm.at[:, :, :, pl.ds(pl.multiple_of(p * HEAD, HEAD), HEAD)],
        held.at[p],
        local_sem.at[2],
    )
    load_table = pltpu.make_async_copy(table_hbm, table_ref, local_sem.at[3])
    load_place = pltpu.make_async_copy(place_hbm, place_ref, local_sem.at[4])
    load_offset = pltpu.make_async_copy(offset_hbm, offset_ref, local_sem.at[5])
    load_place.start()
    load_offset.start()
    load_kv.start()
    load_table.start()
    load_held.start()
    load_q.start()

    barrier = pltpu.get_barrier_semaphore()
    for d in range(1, pools):
        pl.semaphore_signal(barrier, inc=1, device_id=((p + d) % pools, c), device_id_type=MESH)

    def greet(d, _):
        pl.semaphore_signal(barrier, inc=1, device_id=(p, (c + d) % ctxs), device_id_type=MESH)
        return 0

    lax.fori_loop(1, ctxs, greet, 0)

    load_place.wait()
    load_offset.wait()
    row8 = lax.broadcasted_iota(jnp.int32, (8, HEAD), 0)
    place_tile = jnp.full((8, HEAD), -1, jnp.int32)
    offset_tile = jnp.zeros((8, HEAD), jnp.int32)
    for i in range(slots):
        place_tile = jnp.where(row8 == i, place_ref[i], place_tile)
        offset_tile = jnp.where(row8 == i, offset_ref[i], offset_tile)
    meta[c, 0] = place_tile
    meta[c, 1] = offset_tile

    load_table.wait()
    freq = table_ref[2 * rows : 2 * rows + 8, :]
    base = (question_start + c * rows).astype(jnp.float32) * freq
    cos_base = jnp.cos(base)[0:1]
    sin_base = jnp.sin(base)[0:1]
    cos_row = table_ref[:rows]
    sin_row = table_ref[rows : 2 * rows]
    cos_q = cos_row * cos_base - sin_row * sin_base
    sin_q = signed(sin_row * cos_base + cos_row * sin_base)

    load_kv.wait()
    own[c, 0] = turn(kv_raw[0].astype(jnp.float32), cos_q, sin_q).astype(jnp.bfloat16)
    own[c, 1] = kv_raw[1]

    pl.semaphore_wait(barrier, pools - 1 + ctxs - 1)

    def pool_copy(d):
        target = (p + d) % pools
        return pltpu.make_async_remote_copy(
            src_ref=cache_hbm.at[:, :, :, pl.ds(pl.multiple_of(target * HEAD, HEAD), HEAD)],
            dst_ref=held.at[p],
            send_sem=pool_send.at[d],
            recv_sem=pool_recv.at[d],
            device_id=(target, c),
            device_id_type=MESH,
        )

    def meta_copy(d):
        return pltpu.make_async_remote_copy(
            src_ref=meta.at[c],
            dst_ref=meta.at[c],
            send_sem=meta_send.at[d],
            recv_sem=meta_recv.at[d],
            device_id=(p, (c + d) % ctxs),
            device_id_type=MESH,
        )

    def chip_copy(buffer, send, recv, d):
        return pltpu.make_async_remote_copy(
            src_ref=buffer.at[c],
            dst_ref=buffer.at[c],
            send_sem=send.at[d],
            recv_sem=recv.at[d],
            device_id=(p, 2 * flip_chip(t, d, chips) + core),
            device_id_type=MESH,
        )

    def forward_copy(buffer, send, recv, d):
        place = 2 * flip_chip(t, d, chips) + core
        return pltpu.make_async_remote_copy(
            src_ref=buffer.at[place],
            dst_ref=buffer.at[place],
            send_sem=send.at[d],
            recv_sem=recv.at[d],
            device_id=(p, sibling),
            device_id_type=MESH,
        )

    own_sems = (own, own_send, own_recv)
    own_fwd = (own, own_fwd_send, own_fwd_recv)
    pas_sems = (pas, pas_send, pas_recv)
    pas_fwd = (pas, pas_fwd_send, pas_fwd_recv)

    for d in range(1, pools):
        pool_copy(d).start()
    forward_copy(*own_fwd, 0).start()

    def start_meta(d, _):
        meta_copy(d).start()
        return 0

    lax.fori_loop(1, ctxs, start_meta, 0)

    def start_own(d, _):
        @pl.when(flip_chip(t, d, chips) > t)
        def _():
            chip_copy(*own_sems, d).start()

        return 0

    lax.fori_loop(1, chips, start_own, 0)

    load_q.wait()
    for g in range(heads):
        vectors = q_raw[:, g * HEAD : (g + 1) * HEAD].astype(jnp.float32)
        q_rot[g] = turn(vectors, cos_q, sin_q).astype(jnp.bfloat16)

    ones = jnp.ones((2 * shard, HEAD), jnp.bfloat16)

    def attend(keys, first, allowed, between):
        width = keys.shape[0]
        wide = width // HEAD

        def one_head(g, _):
            scores = lax.dot_general(
                q_rot[g], keys[...], (((1,), (1,)), ((), ())), preferred_element_type=jnp.float32
            )
            if allowed is not None:
                scores = jnp.where(allowed(scores.shape), scores, MASKED)
            peak = jnp.broadcast_to(jnp.max(scores, axis=1, keepdims=True), (rows, HEAD))
            if not first:
                before = top[g]
                peak = jnp.maximum(before, peak)
            weights = jnp.exp2((scores - jnp.concatenate([peak] * wide, axis=1)) * LOG2_SCALE)
            product = jnp.dot(
                weights.astype(jnp.bfloat16), v_now[...], preferred_element_type=jnp.float32
            )
            if first:
                acc[g] = product
            else:
                shrink = jnp.exp2((before - peak) * LOG2_SCALE)
                acc[g] = acc[g] * jnp.concatenate([shrink, shrink], axis=1) + product
            top[g] = peak
            return 0

        half = heads // 2
        lax.fori_loop(0, half, one_head, 0, unroll=True)
        between()
        lax.fori_loop(half, heads, one_head, 0, unroll=True)

    def gather_chunk(buffer, chip):
        k_now[...] = buffer[pl.ds(2 * chip, 2), 0].reshape(2 * shard, HEAD)
        v_now[:, :HEAD] = buffer[pl.ds(2 * chip, 2), 1].reshape(2 * shard, HEAD)

    forward_copy(*own_fwd, 0).wait_recv()
    gather_chunk(own, t)
    v_now[:, HEAD:] = ones

    def causal(shape):
        key = lax.broadcasted_iota(jnp.int32, shape, 1)
        query = lax.broadcasted_iota(jnp.int32, shape, 0) + core * rows
        return key <= query

    def own_arrive(d):
        @pl.when(flip_chip(t, d, chips) < t)
        def _():
            chip_copy(*own_sems, d).wait_recv()
            forward_copy(*own_fwd, d).start()

    def pas_arrive(d):
        chip_copy(*pas_sems, d).wait_recv()
        forward_copy(*pas_fwd, d).start()

    attend(k_now, True, causal, lambda: own_arrive(1))

    def own_step(d, _):
        source = flip_chip(t, d, chips)

        def later():
            @pl.when(d + 1 < chips)
            def _():
                own_arrive(d + 1)

        @pl.when(source < t)
        def _():
            forward_copy(*own_fwd, d).wait_recv()
            gather_chunk(own, source)
            attend(k_now, False, None, later)

        @pl.when(source > t)
        def _():
            later()

        return 0

    own_step(1, 0)

    def wait_meta(d, _):
        meta_copy(d).wait_recv()
        return 0

    lax.fori_loop(1, ctxs, wait_meta, 0)
    load_held.wait()
    for d in range(1, pools):
        pool_copy(d).wait_recv()

    places = meta[:, 0]
    offsets = meta[:, 1].astype(jnp.float32)
    live, where_to, rank = [], [], []
    filled = jnp.zeros((1, HEAD), jnp.float32)
    for b in range(pools * hold):
        block_id = ((b // hold) * ctxs + c) * hold + b % hold
        match = jnp.where(places == block_id, 1.0, 0.0)
        live.append(jnp.sum(jnp.sum(match, axis=0), axis=0, keepdims=True))
        where_to.append(jnp.sum(jnp.sum(match * offsets, axis=0), axis=0, keepdims=True))
        rank.append(filled)
        filled = filled + live[-1]
    for k in range(slots):
        key_sum = jnp.zeros((block, HEAD), jnp.float32)
        value_sum = jnp.zeros((block, HEAD), jnp.float32)
        offset = jnp.zeros((1, HEAD), jnp.float32)
        for b in range(pools * hold):
            pick = jnp.where(rank[b] == float(k), live[b], 0.0)
            key_sum = key_sum + pick * held[b // hold, b % hold, 0].astype(jnp.float32)
            value_sum = value_sum + pick * held[b // hold, b % hold, 1].astype(jnp.float32)
            offset = offset + pick * where_to[b]
        angle = offset * freq
        cos_k = jnp.cos(angle)[0:1]
        sin_k = signed(jnp.sin(angle))[0:1]
        pas[c, 0, k * block : (k + 1) * block] = turn(key_sum, cos_k, sin_k).astype(jnp.bfloat16)
        pas[c, 1, k * block : (k + 1) * block] = value_sum.astype(jnp.bfloat16)

    forward_copy(*pas_fwd, 0).start()

    def start_pas(d, _):
        chip_copy(*pas_sems, d).start()
        return 0

    lax.fori_loop(1, chips, start_pas, 0)

    lax.fori_loop(2, chips, own_step, 0)

    hold_bits = hold.bit_length() - 1

    def pas_step(d, _):
        source = flip_chip(t, d, chips)

        forward_copy(*pas_fwd, d).wait_recv()
        v_now[:, :HEAD] = pas[pl.ds(2 * source, 2), 1].reshape(2 * shard, HEAD)
        seen = own[c, 0, 0:16].astype(jnp.float32)[0:1]
        all_places = meta[:, 0]
        holder = lax.shift_right_logical(all_places, hold_bits) & (ctxs - 1)
        for side in range(2):
            column = 2 * source + side
            mine = jnp.where((all_places >= 0) & (holder == column), 1.0, 0.0)
            count = jnp.sum(jnp.sum(mine, axis=0), axis=0, keepdims=True)
            for k in range(slots):
                flag = jnp.broadcast_to(jnp.where(count > float(k), 1.0, 0.0), (block, HEAD))
                at = side * shard + k * block
                keys = pas[column, 0, k * block : (k + 1) * block].astype(jnp.float32)
                k_now[at : at + block] = jnp.where(flag > 0.0, keys, seen).astype(jnp.bfloat16)
                v_now[at : at + block, HEAD:] = flag.astype(jnp.bfloat16)

        def later():
            @pl.when(d + 1 < chips)
            def _():
                pas_arrive(d + 1)

        attend(k_now, False, None, later)
        return 0

    lax.fori_loop(0, chips, pas_step, 0)

    for g in range(heads):
        out_ref[:, g * HEAD : (g + 1) * HEAD] = (
            acc[g, :, :HEAD] / acc[g, :, HEAD:]
        ).astype(jnp.bfloat16)

    for d in range(1, pools):
        pool_copy(d).wait_send()

    def end_meta(d, _):
        meta_copy(d).wait_send()
        return 0

    lax.fori_loop(1, ctxs, end_meta, 0)
    forward_copy(*own_fwd, 0).wait_send()
    forward_copy(*pas_fwd, 0).wait_send()

    def end_chips(d, _):
        other = flip_chip(t, d, chips)

        @pl.when(other > t)
        def _():
            chip_copy(*own_sems, d).wait_send()

        @pl.when(other < t)
        def _():
            forward_copy(*own_fwd, d).wait_send()

        chip_copy(*pas_sems, d).wait_send()
        forward_copy(*pas_fwd, d).wait_send()
        return 0

    lax.fori_loop(1, chips, end_chips, 0)


def shards(counts, question_q, question_kv, cache_kv, placement, offsets):
    pools, ctxs = counts
    chips = ctxs // 2
    rows, width = question_q.shape
    heads = width // HEAD
    hold, _, block, _ = cache_kv.shape
    slots = placement.shape[0]
    shard = slots * block
    dma = pltpu.SemaphoreType.DMA
    any_space = pl.BlockSpec(memory_space=pl.ANY)
    return pl.pallas_call(
        functools.partial(kernel, counts),
        out_shape=jax.ShapeDtypeStruct((rows, width), jnp.bfloat16),
        in_specs=[
            any_space,
            any_space,
            any_space,
            any_space,
            any_space,
            any_space,
        ],
        out_specs=pl.BlockSpec(memory_space=pltpu.VMEM),
        scratch_shapes=[
            pltpu.SMEM((slots,), jnp.int32),
            pltpu.SMEM((slots,), jnp.int32),
            pltpu.VMEM((2 * rows + 8, HEAD), jnp.float32),
            pltpu.VMEM((rows, width), jnp.bfloat16),
            pltpu.VMEM((heads, rows, HEAD), jnp.bfloat16),
            pltpu.VMEM((2, rows, HEAD), jnp.bfloat16),
            pltpu.VMEM((ctxs, 2, rows, HEAD), jnp.bfloat16),
            pltpu.VMEM((ctxs, 2, shard, HEAD), jnp.bfloat16),
            pltpu.VMEM((pools, hold, 2, block, HEAD), jnp.bfloat16),
            pltpu.VMEM((ctxs, 2, 8, HEAD), jnp.int32),
            pltpu.VMEM((2 * shard, HEAD), jnp.bfloat16),
            pltpu.VMEM((2 * shard, 2 * HEAD), jnp.bfloat16),
            pltpu.VMEM((heads, rows, HEAD), jnp.float32),
            pltpu.VMEM((heads, rows, 2 * HEAD), jnp.float32),
            dma((6,)),
            dma((pools,)),
            dma((pools,)),
            dma((ctxs,)),
            dma((ctxs,)),
            dma((chips,)),
            dma((chips,)),
            dma((chips,)),
            dma((chips,)),
            dma((chips,)),
            dma((chips,)),
            dma((chips,)),
            dma((chips,)),
        ],
        compiler_params=pltpu.CompilerParams(
            collective_id=0, has_side_effects=True, vmem_limit_bytes=60 * 1024 * 1024
        ),
        name="attend_question",
    )(question_q, question_kv, cache_kv, placement, offsets, jnp.asarray(angle_tables(rows)))


def solution(mesh):
    counts = (mesh.shape["pool"], mesh.shape["ctx"])
    in_specs = (
        P("ctx", "pool"),
        P(None, "ctx", "pool"),
        P(("pool", "ctx"), None, None, None),
        P("ctx"),
        P("ctx"),
    )
    return jax.shard_map(
        functools.partial(shards, counts),
        mesh=mesh,
        in_specs=in_specs,
        out_specs=P("ctx", "pool"),
        check_vma=False,
    )
```

```python
import functools
import math

import jax
import jax.numpy as jnp
import numpy as np
from jax import lax
from jax.experimental import pallas as pl
from jax.experimental.pallas import tpu as pltpu
from jax.sharding import PartitionSpec as P

HEAD = 128
HALF = HEAD // 2
ROPE_BASE = 500000.0
MASKED = -1e30
LOG2_SCALE = HEAD**-0.5 * math.log2(math.e)
MESH = pl.DeviceIdType.MESH


def angle_tables(rows):
    frequency = ROPE_BASE ** (-np.arange(HALF, dtype=np.float64) / HALF)
    frequency = np.concatenate([frequency, frequency])
    angles = np.arange(rows)[:, None] * frequency[None, :]
    parts = [np.cos(angles), np.sin(angles), np.tile(frequency[None, :], (8, 1))]
    return np.concatenate(parts).astype(np.float32)


def flip_chip(chip, step, chips):
    result, bit = 0, 1
    while bit < chips:
        a = (chip // bit) % 2
        b = (step // bit) % 2
        result = result + bit * (a + b - 2 * a * b)
        bit *= 2
    return result


def signed(sine):
    lane = lax.broadcasted_iota(jnp.int32, sine.shape, 1)
    return jnp.where(lane < HALF, -sine, sine)


def turn(vectors, cosine, sine_signed):
    return vectors * cosine + pltpu.roll(vectors, HALF, 1) * sine_signed


def kernel(
    counts,
    q_hbm,
    kv_hbm,
    cache_hbm,
    place_hbm,
    offset_hbm,
    table_hbm,
    out_ref,
    place_ref,
    offset_ref,
    table_ref,
    q_raw,
    q_rot,
    kv_raw,
    own,
    pas,
    held,
    meta,
    k_now,
    v_now,
    top,
    acc,
    local_sem,
    pool_send,
    pool_recv,
    meta_send,
    meta_recv,
    own_send,
    own_recv,
    own_fwd_send,
    own_fwd_recv,
    pas_send,
    pas_recv,
    pas_fwd_send,
    pas_fwd_recv,
):
    pools, ctxs = counts
    chips = ctxs // 2
    p = lax.axis_index("pool")
    c = lax.axis_index("ctx")
    t = c // 2
    core = c % 2
    sibling = 2 * t + 1 - core
    rows = q_raw.shape[0]
    heads = q_rot.shape[0]
    hold = held.shape[1]
    block = held.shape[3]
    slots = place_ref.shape[0]
    shard = slots * block
    question_start = ctxs * slots * block

    load_q = pltpu.make_async_copy(q_hbm, q_raw, local_sem.at[0])
    load_kv = pltpu.make_async_copy(kv_hbm, kv_raw, local_sem.at[1])
    load_held = pltpu.make_async_copy(
        cache_hbm.at[:, :, :, pl.ds(pl.multiple_of(p * HEAD, HEAD), HEAD)],
        held.at[p],
        local_sem.at[2],
    )
    load_table = pltpu.make_async_copy(table_hbm, table_ref, local_sem.at[3])
    load_place = pltpu.make_async_copy(place_hbm, place_ref, local_sem.at[4])
    load_offset = pltpu.make_async_copy(offset_hbm, offset_ref, local_sem.at[5])
    load_place.start()
    load_offset.start()
    load_kv.start()
    load_table.start()
    load_held.start()
    load_q.start()

    barrier = pltpu.get_barrier_semaphore()
    for d in range(1, pools):
        pl.semaphore_signal(barrier, inc=1, device_id=((p + d) % pools, c), device_id_type=MESH)

    def greet(d, _):
        pl.semaphore_signal(barrier, inc=1, device_id=(p, (c + d) % ctxs), device_id_type=MESH)
        return 0

    lax.fori_loop(1, ctxs, greet, 0)

    load_place.wait()
    load_offset.wait()
    row8 = lax.broadcasted_iota(jnp.int32, (8, HEAD), 0)
    place_tile = jnp.full((8, HEAD), -1, jnp.int32)
    offset_tile = jnp.zeros((8, HEAD), jnp.int32)
    for i in range(slots):
        place_tile = jnp.where(row8 == i, place_ref[i], place_tile)
        offset_tile = jnp.where(row8 == i, offset_ref[i], offset_tile)
    meta[c, 0] = place_tile
    meta[c, 1] = offset_tile

    load_table.wait()
    freq = table_ref[2 * rows : 2 * rows + 8, :]
    base = (question_start + c * rows).astype(jnp.float32) * freq
    cos_base = jnp.cos(base)[0:1]
    sin_base = jnp.sin(base)[0:1]
    cos_row = table_ref[:rows]
    sin_row = table_ref[rows : 2 * rows]
    cos_q = cos_row * cos_base - sin_row * sin_base
    sin_q = signed(sin_row * cos_base + cos_row * sin_base)

    load_kv.wait()
    turned = turn(kv_raw[0].astype(jnp.float32), cos_q, sin_q)
    for j in range(rows // HEAD):
        tile = turned[j * HEAD : (j + 1) * HEAD]
        own[c, 0, j * HEAD : (j + 1) * HEAD] = tile.T.astype(jnp.bfloat16)
    own[c, 1] = kv_raw[1]

    pl.semaphore_wait(barrier, pools - 1 + ctxs - 1)

    def pool_copy(d):
        target = (p + d) % pools
        return pltpu.make_async_remote_copy(
            src_ref=cache_hbm.at[:, :, :, pl.ds(pl.multiple_of(target * HEAD, HEAD), HEAD)],
            dst_ref=held.at[p],
            send_sem=pool_send.at[d],
            recv_sem=pool_recv.at[d],
            device_id=(target, c),
            device_id_type=MESH,
        )

    def meta_copy(d):
        return pltpu.make_async_remote_copy(
            src_ref=meta.at[c],
            dst_ref=meta.at[c],
            send_sem=meta_send.at[d],
            recv_sem=meta_recv.at[d],
            device_id=(p, (c + d) % ctxs),
            device_id_type=MESH,
        )

    def chip_copy(buffer, send, recv, d):
        return pltpu.make_async_remote_copy(
            src_ref=buffer.at[c],
            dst_ref=buffer.at[c],
            send_sem=send.at[d],
            recv_sem=recv.at[d],
            device_id=(p, 2 * flip_chip(t, d, chips) + core),
            device_id_type=MESH,
        )

    def forward_copy(buffer, send, recv, d):
        place = 2 * flip_chip(t, d, chips) + core
        return pltpu.make_async_remote_copy(
            src_ref=buffer.at[place],
            dst_ref=buffer.at[place],
            send_sem=send.at[d],
            recv_sem=recv.at[d],
            device_id=(p, sibling),
            device_id_type=MESH,
        )

    own_sems = (own, own_send, own_recv)
    own_fwd = (own, own_fwd_send, own_fwd_recv)
    pas_sems = (pas, pas_send, pas_recv)
    pas_fwd = (pas, pas_fwd_send, pas_fwd_recv)

    for d in range(1, pools):
        pool_copy(d).start()
    forward_copy(*own_fwd, 0).start()

    def start_meta(d, _):
        meta_copy(d).start()
        return 0

    lax.fori_loop(1, ctxs, start_meta, 0)

    def start_own(d, _):
        @pl.when(flip_chip(t, d, chips) > t)
        def _():
            chip_copy(*own_sems, d).start()

        return 0

    lax.fori_loop(1, chips, start_own, 0)

    load_q.wait()
    for g in range(heads):
        vectors = q_raw[:, g * HEAD : (g + 1) * HEAD].astype(jnp.float32)
        q_rot[g] = turn(vectors, cos_q, sin_q).astype(jnp.bfloat16)

    ones = jnp.ones((2 * shard, HEAD), jnp.bfloat16)

    def attend(first):
        width = k_now.shape[1]
        wide = width // HEAD
        scores = jnp.dot(
            q_rot[...].reshape(heads * rows, HEAD), k_now[...], preferred_element_type=jnp.float32
        )
        if first:
            key = lax.broadcasted_iota(jnp.int32, (heads, rows, width), 2)
            query = lax.broadcasted_iota(jnp.int32, (heads, rows, width), 1) + core * rows
            scores = jnp.where((key <= query).reshape(scores.shape), scores, MASKED)
        peak = jnp.broadcast_to(jnp.max(scores, axis=1, keepdims=True), (heads * rows, HEAD))
        if not first:
            before = top[...]
            peak = jnp.maximum(before, peak)
        weights = jnp.exp2((scores - jnp.concatenate([peak] * wide, axis=1)) * LOG2_SCALE)
        product = jnp.dot(
            weights.astype(jnp.bfloat16), v_now[...], preferred_element_type=jnp.float32
        )
        if first:
            acc[...] = product
        else:
            shrink = jnp.exp2((before - peak) * LOG2_SCALE)
            acc[...] = acc[...] * jnp.concatenate([shrink, shrink], axis=1) + product
        top[...] = peak

    def gather_chunk(buffer, chip):
        for side in range(2):
            for j in range(shard // HEAD):
                at = side * shard + j * HEAD
                k_now[:, at : at + HEAD] = buffer[2 * chip + side, 0, j * HEAD : (j + 1) * HEAD]
        v_now[:, :HEAD] = buffer[pl.ds(2 * chip, 2), 1].reshape(2 * shard, HEAD)

    forward_copy(*own_fwd, 0).wait_recv()
    gather_chunk(own, t)
    v_now[:, HEAD:] = ones

    def own_arrive(d):
        @pl.when(flip_chip(t, d, chips) < t)
        def _():
            chip_copy(*own_sems, d).wait_recv()
            forward_copy(*own_fwd, d).start()

    def pas_arrive(d):
        chip_copy(*pas_sems, d).wait_recv()
        forward_copy(*pas_fwd, d).start()

    own_arrive(1)
    attend(True)

    def own_step(d, _):
        source = flip_chip(t, d, chips)

        def later():
            @pl.when(d + 1 < chips)
            def _():
                own_arrive(d + 1)

        @pl.when(source < t)
        def _():
            forward_copy(*own_fwd, d).wait_recv()
            gather_chunk(own, source)
            later()
            attend(False)

        @pl.when(source > t)
        def _():
            later()

        return 0

    own_step(1, 0)

    def wait_meta(d, _):
        meta_copy(d).wait_recv()
        return 0

    lax.fori_loop(1, ctxs, wait_meta, 0)
    load_held.wait()
    for d in range(1, pools):
        pool_copy(d).wait_recv()

    places = meta[:, 0]
    offsets = meta[:, 1].astype(jnp.float32)
    live, where_to, rank = [], [], []
    filled = jnp.zeros((1, HEAD), jnp.float32)
    for b in range(pools * hold):
        block_id = ((b // hold) * ctxs + c) * hold + b % hold
        match = jnp.where(places == block_id, 1.0, 0.0)
        live.append(jnp.sum(jnp.sum(match, axis=0), axis=0, keepdims=True))
        where_to.append(jnp.sum(jnp.sum(match * offsets, axis=0), axis=0, keepdims=True))
        rank.append(filled)
        filled = filled + live[-1]
    turned_keys = []
    for k in range(slots):
        key_sum = jnp.zeros((block, HEAD), jnp.float32)
        value_sum = jnp.zeros((block, HEAD), jnp.float32)
        offset = jnp.zeros((1, HEAD), jnp.float32)
        for b in range(pools * hold):
            pick = jnp.where(rank[b] == float(k), live[b], 0.0)
            key_sum = key_sum + pick * held[b // hold, b % hold, 0].astype(jnp.float32)
            value_sum = value_sum + pick * held[b // hold, b % hold, 1].astype(jnp.float32)
            offset = offset + pick * where_to[b]
        angle = offset * freq
        cos_k = jnp.cos(angle)[0:1]
        sin_k = signed(jnp.sin(angle))[0:1]
        turned_keys.append(turn(key_sum, cos_k, sin_k))
        pas[c, 1, k * block : (k + 1) * block] = value_sum.astype(jnp.bfloat16)

    turned = jnp.concatenate(turned_keys, axis=0)
    for j in range(shard // HEAD):
        tile = turned[j * HEAD : (j + 1) * HEAD]
        pas[c, 0, j * HEAD : (j + 1) * HEAD] = tile.T.astype(jnp.bfloat16)

    forward_copy(*pas_fwd, 0).start()

    def start_pas(d, _):
        chip_copy(*pas_sems, d).start()
        return 0

    lax.fori_loop(1, chips, start_pas, 0)

    lax.fori_loop(2, chips, own_step, 0)

    hold_bits = hold.bit_length() - 1

    def pas_step(d, _):
        source = flip_chip(t, d, chips)

        forward_copy(*pas_fwd, d).wait_recv()
        v_now[:, :HEAD] = pas[pl.ds(2 * source, 2), 1].reshape(2 * shard, HEAD)
        seen = jnp.broadcast_to(own[c, 0, 0:HEAD, 0:1].astype(jnp.float32), (HEAD, HEAD))
        lane_slot = lax.broadcasted_iota(jnp.int32, (1, HEAD), 1) // block
        all_places = meta[:, 0]
        holder = lax.shift_right_logical(all_places, hold_bits) & (ctxs - 1)
        for side in range(2):
            column = 2 * source + side
            mine = jnp.where((all_places >= 0) & (holder == column), 1.0, 0.0)
            count = jnp.sum(jnp.sum(mine, axis=0), axis=0, keepdims=True)
            for k in range(slots):
                flag = jnp.broadcast_to(jnp.where(count > float(k), 1.0, 0.0), (block, HEAD))
                at = side * shard + k * block
                v_now[at : at + block, HEAD:] = flag.astype(jnp.bfloat16)

            for j in range(shard // HEAD):
                at = side * shard + j * HEAD
                slot = (lane_slot + j * (HEAD // block)).astype(jnp.float32)
                flag = jnp.broadcast_to(jnp.where(count > slot, 1.0, 0.0), (HEAD, HEAD))
                keys = pas[column, 0, j * HEAD : (j + 1) * HEAD].astype(jnp.float32)
                k_now[:, at : at + HEAD] = jnp.where(flag > 0.0, keys, seen).astype(jnp.bfloat16)

        def later():
            @pl.when(d + 1 < chips)
            def _():
                pas_arrive(d + 1)

        later()
        attend(False)
        return 0

    lax.fori_loop(0, chips, pas_step, 0)

    for g in range(heads):
        part = acc[g * rows : (g + 1) * rows]
        out_ref[:, g * HEAD : (g + 1) * HEAD] = (part[:, :HEAD] / part[:, HEAD:]).astype(
            jnp.bfloat16
        )

    for d in range(1, pools):
        pool_copy(d).wait_send()

    def end_meta(d, _):
        meta_copy(d).wait_send()
        return 0

    lax.fori_loop(1, ctxs, end_meta, 0)
    forward_copy(*own_fwd, 0).wait_send()
    forward_copy(*pas_fwd, 0).wait_send()

    def end_chips(d, _):
        other = flip_chip(t, d, chips)

        @pl.when(other > t)
        def _():
            chip_copy(*own_sems, d).wait_send()

        @pl.when(other < t)
        def _():
            forward_copy(*own_fwd, d).wait_send()

        chip_copy(*pas_sems, d).wait_send()
        forward_copy(*pas_fwd, d).wait_send()
        return 0

    lax.fori_loop(1, chips, end_chips, 0)


def shards(counts, question_q, question_kv, cache_kv, placement, offsets):
    pools, ctxs = counts
    chips = ctxs // 2
    rows, width = question_q.shape
    heads = width // HEAD
    hold, _, block, _ = cache_kv.shape
    slots = placement.shape[0]
    shard = slots * block
    dma = pltpu.SemaphoreType.DMA
    any_space = pl.BlockSpec(memory_space=pltpu.HBM)
    return pl.pallas_call(
        functools.partial(kernel, counts),
        out_shape=jax.ShapeDtypeStruct((rows, width), jnp.bfloat16),
        in_specs=[
            any_space,
            any_space,
            any_space,
            any_space,
            any_space,
            any_space,
        ],
        out_specs=pl.BlockSpec(memory_space=pltpu.VMEM),
        scratch_shapes=[
            pltpu.SMEM((slots,), jnp.int32),
            pltpu.SMEM((slots,), jnp.int32),
            pltpu.VMEM((2 * rows + 8, HEAD), jnp.float32),
            pltpu.VMEM((rows, width), jnp.bfloat16),
            pltpu.VMEM((heads, rows, HEAD), jnp.bfloat16),
            pltpu.VMEM((2, rows, HEAD), jnp.bfloat16),
            pltpu.VMEM((ctxs, 2, rows, HEAD), jnp.bfloat16),
            pltpu.VMEM((ctxs, 2, shard, HEAD), jnp.bfloat16),
            pltpu.VMEM((pools, hold, 2, block, HEAD), jnp.bfloat16),
            pltpu.VMEM((ctxs, 2, 8, HEAD), jnp.int32),
            pltpu.VMEM((HEAD, 2 * shard), jnp.bfloat16),
            pltpu.VMEM((2 * shard, 2 * HEAD), jnp.bfloat16),
            pltpu.VMEM((heads * rows, HEAD), jnp.float32),
            pltpu.VMEM((heads * rows, 2 * HEAD), jnp.float32),
            dma((6,)),
            dma((pools,)),
            dma((pools,)),
            dma((ctxs,)),
            dma((ctxs,)),
            dma((chips,)),
            dma((chips,)),
            dma((chips,)),
            dma((chips,)),
            dma((chips,)),
            dma((chips,)),
            dma((chips,)),
            dma((chips,)),
        ],
        compiler_params=pltpu.CompilerParams(
            collective_id=0, has_side_effects=True, vmem_limit_bytes=60 * 1024 * 1024
        ),
        name="attend_question",
    )(question_q, question_kv, cache_kv, placement, offsets, jnp.asarray(angle_tables(rows)))


def solution(mesh):
    counts = (mesh.shape["pool"], mesh.shape["ctx"])
    in_specs = (
        P("ctx", "pool"),
        P(None, "ctx", "pool"),
        P(("pool", "ctx"), None, None, None),
        P("ctx"),
        P("ctx"),
    )
    return jax.shard_map(
        functools.partial(shards, counts),
        mesh=mesh,
        in_specs=in_specs,
        out_specs=P("ctx", "pool"),
        check_vma=False,
    )
```

```python
import functools
import math

import jax
import jax.numpy as jnp
import numpy as np
from jax import lax
from jax.experimental import pallas as pl
from jax.experimental.pallas import tpu as pltpu
from jax.sharding import PartitionSpec as P

HEAD = 128
HALF = HEAD // 2
ROPE_BASE = 500000.0
MASKED = -1e30
LOG2_SCALE = HEAD**-0.5 * math.log2(math.e)
MESH = pl.DeviceIdType.MESH


def angle_tables(rows):
    frequency = ROPE_BASE ** (-np.arange(HALF, dtype=np.float64) / HALF)
    frequency = np.concatenate([frequency, frequency])
    angles = np.arange(rows)[:, None] * frequency[None, :]
    parts = [np.cos(angles), np.sin(angles), np.tile(frequency[None, :], (8, 1))]
    return np.concatenate(parts).astype(np.float32)


def flip_chip(chip, step, chips):
    result, bit = 0, 1
    while bit < chips:
        a = (chip // bit) % 2
        b = (step // bit) % 2
        result = result + bit * (a + b - 2 * a * b)
        bit *= 2
    return result


def signed(sine):
    lane = lax.broadcasted_iota(jnp.int32, sine.shape, 1)
    return jnp.where(lane < HALF, -sine, sine)


def turn(vectors, cosine, sine_signed):
    return vectors * cosine + pltpu.roll(vectors, HALF, 1) * sine_signed


def kernel(
    counts,
    q_hbm,
    kv_hbm,
    cache_hbm,
    place_hbm,
    offset_hbm,
    table_hbm,
    out_ref,
    place_ref,
    offset_ref,
    table_ref,
    q_raw,
    q_rot,
    kv_raw,
    own,
    pas,
    held,
    meta,
    k_now,
    v_now,
    top,
    acc,
    local_sem,
    pool_send,
    pool_recv,
    meta_send,
    meta_recv,
    own_send,
    own_recv,
    own_fwd_send,
    own_fwd_recv,
    pas_send,
    pas_recv,
    pas_fwd_send,
    pas_fwd_recv,
):
    pools, ctxs = counts
    chips = ctxs // 2
    p = lax.axis_index("pool")
    c = lax.axis_index("ctx")
    t = c // 2
    core = c % 2
    sibling = 2 * t + 1 - core
    rows = q_raw.shape[0]
    heads = q_rot.shape[0]
    hold = held.shape[1]
    block = held.shape[3]
    slots = place_ref.shape[0]
    shard = slots * block
    question_start = ctxs * slots * block

    load_q = pltpu.make_async_copy(q_hbm, q_raw, local_sem.at[0])
    load_kv = pltpu.make_async_copy(kv_hbm, kv_raw, local_sem.at[1])
    load_held = pltpu.make_async_copy(
        cache_hbm.at[:, :, :, pl.ds(pl.multiple_of(p * HEAD, HEAD), HEAD)],
        held.at[p],
        local_sem.at[2],
    )
    load_table = pltpu.make_async_copy(table_hbm, table_ref, local_sem.at[3])
    load_place = pltpu.make_async_copy(place_hbm, place_ref, local_sem.at[4])
    load_offset = pltpu.make_async_copy(offset_hbm, offset_ref, local_sem.at[5])
    load_place.start()
    load_offset.start()
    load_kv.start()
    load_table.start()
    load_held.start()
    load_q.start()

    barrier = pltpu.get_barrier_semaphore()
    for d in range(1, pools):
        pl.semaphore_signal(barrier, inc=1, device_id=((p + d) % pools, c), device_id_type=MESH)

    def greet(d, _):
        pl.semaphore_signal(barrier, inc=1, device_id=(p, (c + d) % ctxs), device_id_type=MESH)
        return 0

    lax.fori_loop(1, ctxs, greet, 0)

    load_place.wait()
    load_offset.wait()
    row8 = lax.broadcasted_iota(jnp.int32, (8, HEAD), 0)
    place_tile = jnp.full((8, HEAD), -1, jnp.int32)
    offset_tile = jnp.zeros((8, HEAD), jnp.int32)
    for i in range(slots):
        place_tile = jnp.where(row8 == i, place_ref[i], place_tile)
        offset_tile = jnp.where(row8 == i, offset_ref[i], offset_tile)
    meta[c, 0] = place_tile
    meta[c, 1] = offset_tile

    load_table.wait()
    freq = table_ref[2 * rows : 2 * rows + 8, :]
    base = (question_start + c * rows).astype(jnp.float32) * freq
    cos_base = jnp.cos(base)[0:1]
    sin_base = jnp.sin(base)[0:1]
    cos_row = table_ref[:rows]
    sin_row = table_ref[rows : 2 * rows]
    cos_q = cos_row * cos_base - sin_row * sin_base
    sin_q = signed(sin_row * cos_base + cos_row * sin_base)

    load_kv.wait()
    turned = turn(kv_raw[0].astype(jnp.float32), cos_q, sin_q)
    for j in range(rows // HEAD):
        tile = turned[j * HEAD : (j + 1) * HEAD]
        own[c, 0, j * HEAD : (j + 1) * HEAD] = tile.T.astype(jnp.bfloat16)
    own[c, 1] = kv_raw[1]

    pl.semaphore_wait(barrier, pools - 1 + ctxs - 1)

    def pool_copy(d):
        target = (p + d) % pools
        return pltpu.make_async_remote_copy(
            src_ref=cache_hbm.at[:, :, :, pl.ds(pl.multiple_of(target * HEAD, HEAD), HEAD)],
            dst_ref=held.at[p],
            send_sem=pool_send.at[d],
            recv_sem=pool_recv.at[d],
            device_id=(target, c),
            device_id_type=MESH,
        )

    def meta_copy(d):
        return pltpu.make_async_remote_copy(
            src_ref=meta.at[c],
            dst_ref=meta.at[c],
            send_sem=meta_send.at[d],
            recv_sem=meta_recv.at[d],
            device_id=(p, (c + d) % ctxs),
            device_id_type=MESH,
        )

    def chip_copy(buffer, send, recv, d):
        return pltpu.make_async_remote_copy(
            src_ref=buffer.at[c],
            dst_ref=buffer.at[c],
            send_sem=send.at[d],
            recv_sem=recv.at[d],
            device_id=(p, 2 * flip_chip(t, d, chips) + core),
            device_id_type=MESH,
        )

    def forward_copy(buffer, send, recv, d):
        place = 2 * flip_chip(t, d, chips) + core
        return pltpu.make_async_remote_copy(
            src_ref=buffer.at[place],
            dst_ref=buffer.at[place],
            send_sem=send.at[d],
            recv_sem=recv.at[d],
            device_id=(p, sibling),
            device_id_type=MESH,
        )

    own_sems = (own, own_send, own_recv)
    own_fwd = (own, own_fwd_send, own_fwd_recv)
    pas_sems = (pas, pas_send, pas_recv)
    pas_fwd = (pas, pas_fwd_send, pas_fwd_recv)

    for d in range(1, pools):
        pool_copy(d).start()
    forward_copy(*own_fwd, 0).start()

    def start_meta(d, _):
        meta_copy(d).start()
        return 0

    lax.fori_loop(1, ctxs, start_meta, 0)

    def start_own(d, _):
        @pl.when(flip_chip(t, d, chips) > t)
        def _():
            chip_copy(*own_sems, d).start()

        return 0

    lax.fori_loop(1, chips, start_own, 0)

    load_q.wait()
    for g in range(heads):
        vectors = q_raw[:, g * HEAD : (g + 1) * HEAD].astype(jnp.float32)
        q_rot[g] = turn(vectors, cos_q, sin_q).astype(jnp.bfloat16)

    ones = jnp.ones((2 * shard, HEAD), jnp.bfloat16)

    def attend(first):
        width = k_now.shape[1]
        wide = width // HEAD
        scores = jnp.dot(
            q_rot[...].reshape(heads * rows, HEAD), k_now[...], preferred_element_type=jnp.float32
        )
        if first:
            key = lax.broadcasted_iota(jnp.int32, (heads, rows, width), 2)
            query = lax.broadcasted_iota(jnp.int32, (heads, rows, width), 1) + core * rows
            scores = jnp.where((key <= query).reshape(scores.shape), scores, MASKED)
        peak = jnp.broadcast_to(jnp.max(scores, axis=1, keepdims=True), (heads * rows, HEAD))
        if not first:
            before = top[...]
            peak = jnp.maximum(before, peak)
        weights = jnp.exp2((scores - jnp.concatenate([peak] * wide, axis=1)) * LOG2_SCALE)
        product = jnp.dot(
            weights.astype(jnp.bfloat16), v_now[...], preferred_element_type=jnp.float32
        )
        if first:
            acc[...] = product
        else:
            shrink = jnp.exp2((before - peak) * LOG2_SCALE)
            acc[...] = acc[...] * jnp.concatenate([shrink, shrink], axis=1) + product
        top[...] = peak

    def gather_chunk(buffer, chip):
        for side in range(2):
            for j in range(shard // HEAD):
                at = side * shard + j * HEAD
                k_now[:, at : at + HEAD] = buffer[2 * chip + side, 0, j * HEAD : (j + 1) * HEAD]
        v_now[:, :HEAD] = buffer[pl.ds(2 * chip, 2), 1].reshape(2 * shard, HEAD)

    forward_copy(*own_fwd, 0).wait_recv()
    gather_chunk(own, t)
    v_now[:, HEAD:] = ones

    def own_arrive(d):
        @pl.when(flip_chip(t, d, chips) < t)
        def _():
            chip_copy(*own_sems, d).wait_recv()
            forward_copy(*own_fwd, d).start()

    def pas_arrive(d):
        chip_copy(*pas_sems, d).wait_recv()
        forward_copy(*pas_fwd, d).start()

    attend(True)
    own_arrive(1)

    def own_step(d, _):
        source = flip_chip(t, d, chips)

        def later():
            @pl.when(d + 1 < chips)
            def _():
                own_arrive(d + 1)

        @pl.when(source < t)
        def _():
            forward_copy(*own_fwd, d).wait_recv()
            gather_chunk(own, source)
            later()
            attend(False)

        @pl.when(source > t)
        def _():
            later()

        return 0

    def wait_meta(d, _):
        meta_copy(d).wait_recv()
        return 0

    lax.fori_loop(1, ctxs, wait_meta, 0)
    load_held.wait()
    for d in range(1, pools):
        pool_copy(d).wait_recv()

    places = meta[:, 0]
    offsets = meta[:, 1].astype(jnp.float32)
    live, where_to, rank = [], [], []
    filled = jnp.zeros((1, HEAD), jnp.float32)
    for b in range(pools * hold):
        block_id = ((b // hold) * ctxs + c) * hold + b % hold
        match = jnp.where(places == block_id, 1.0, 0.0)
        live.append(jnp.sum(jnp.sum(match, axis=0), axis=0, keepdims=True))
        where_to.append(jnp.sum(jnp.sum(match * offsets, axis=0), axis=0, keepdims=True))
        rank.append(filled)
        filled = filled + live[-1]
    turned_keys = []
    for k in range(slots):
        key_sum = jnp.zeros((block, HEAD), jnp.float32)
        value_sum = jnp.zeros((block, HEAD), jnp.float32)
        offset = jnp.zeros((1, HEAD), jnp.float32)
        for b in range(pools * hold):
            pick = jnp.where(rank[b] == float(k), live[b], 0.0)
            key_sum = key_sum + pick * held[b // hold, b % hold, 0].astype(jnp.float32)
            value_sum = value_sum + pick * held[b // hold, b % hold, 1].astype(jnp.float32)
            offset = offset + pick * where_to[b]
        angle = offset * freq
        cos_k = jnp.cos(angle)[0:1]
        sin_k = signed(jnp.sin(angle))[0:1]
        turned_keys.append(turn(key_sum, cos_k, sin_k))
        pas[c, 1, k * block : (k + 1) * block] = value_sum.astype(jnp.bfloat16)

    turned = jnp.concatenate(turned_keys, axis=0)
    for j in range(shard // HEAD):
        tile = turned[j * HEAD : (j + 1) * HEAD]
        pas[c, 0, j * HEAD : (j + 1) * HEAD] = tile.T.astype(jnp.bfloat16)

    forward_copy(*pas_fwd, 0).start()

    def start_pas(d, _):
        chip_copy(*pas_sems, d).start()
        return 0

    lax.fori_loop(1, chips, start_pas, 0)

    lax.fori_loop(1, chips, own_step, 0)

    hold_bits = hold.bit_length() - 1

    def pas_step(d, _):
        source = flip_chip(t, d, chips)

        forward_copy(*pas_fwd, d).wait_recv()
        v_now[:, :HEAD] = pas[pl.ds(2 * source, 2), 1].reshape(2 * shard, HEAD)
        seen = jnp.broadcast_to(own[c, 0, 0:HEAD, 0:1].astype(jnp.float32), (HEAD, HEAD))
        lane_slot = lax.broadcasted_iota(jnp.int32, (1, HEAD), 1) // block
        all_places = meta[:, 0]
        holder = lax.shift_right_logical(all_places, hold_bits) & (ctxs - 1)
        for side in range(2):
            column = 2 * source + side
            mine = jnp.where((all_places >= 0) & (holder == column), 1.0, 0.0)
            count = jnp.sum(jnp.sum(mine, axis=0), axis=0, keepdims=True)
            for k in range(slots):
                flag = jnp.broadcast_to(jnp.where(count > float(k), 1.0, 0.0), (block, HEAD))
                at = side * shard + k * block
                v_now[at : at + block, HEAD:] = flag.astype(jnp.bfloat16)

            for j in range(shard // HEAD):
                at = side * shard + j * HEAD
                slot = (lane_slot + j * (HEAD // block)).astype(jnp.float32)
                flag = jnp.broadcast_to(jnp.where(count > slot, 1.0, 0.0), (HEAD, HEAD))
                keys = pas[column, 0, j * HEAD : (j + 1) * HEAD].astype(jnp.float32)
                k_now[:, at : at + HEAD] = jnp.where(flag > 0.0, keys, seen).astype(jnp.bfloat16)

        def later():
            @pl.when(d + 1 < chips)
            def _():
                pas_arrive(d + 1)

        later()
        attend(False)
        return 0

    lax.fori_loop(0, chips, pas_step, 0)

    for g in range(heads):
        part = acc[g * rows : (g + 1) * rows]
        out_ref[:, g * HEAD : (g + 1) * HEAD] = (part[:, :HEAD] / part[:, HEAD:]).astype(
            jnp.bfloat16
        )

    for d in range(1, pools):
        pool_copy(d).wait_send()

    def end_meta(d, _):
        meta_copy(d).wait_send()
        return 0

    lax.fori_loop(1, ctxs, end_meta, 0)
    forward_copy(*own_fwd, 0).wait_send()
    forward_copy(*pas_fwd, 0).wait_send()

    def end_chips(d, _):
        other = flip_chip(t, d, chips)

        @pl.when(other > t)
        def _():
            chip_copy(*own_sems, d).wait_send()

        @pl.when(other < t)
        def _():
            forward_copy(*own_fwd, d).wait_send()

        chip_copy(*pas_sems, d).wait_send()
        forward_copy(*pas_fwd, d).wait_send()
        return 0

    lax.fori_loop(1, chips, end_chips, 0)


def shards(counts, question_q, question_kv, cache_kv, placement, offsets):
    pools, ctxs = counts
    chips = ctxs // 2
    rows, width = question_q.shape
    heads = width // HEAD
    hold, _, block, _ = cache_kv.shape
    slots = placement.shape[0]
    shard = slots * block
    dma = pltpu.SemaphoreType.DMA
    any_space = pl.BlockSpec(memory_space=pltpu.HBM)
    return pl.pallas_call(
        functools.partial(kernel, counts),
        out_shape=jax.ShapeDtypeStruct((rows, width), jnp.bfloat16),
        in_specs=[
            any_space,
            any_space,
            any_space,
            any_space,
            any_space,
            any_space,
        ],
        out_specs=pl.BlockSpec(memory_space=pltpu.VMEM),
        scratch_shapes=[
            pltpu.SMEM((slots,), jnp.int32),
            pltpu.SMEM((slots,), jnp.int32),
            pltpu.VMEM((2 * rows + 8, HEAD), jnp.float32),
            pltpu.VMEM((rows, width), jnp.bfloat16),
            pltpu.VMEM((heads, rows, HEAD), jnp.bfloat16),
            pltpu.VMEM((2, rows, HEAD), jnp.bfloat16),
            pltpu.VMEM((ctxs, 2, rows, HEAD), jnp.bfloat16),
            pltpu.VMEM((ctxs, 2, shard, HEAD), jnp.bfloat16),
            pltpu.VMEM((pools, hold, 2, block, HEAD), jnp.bfloat16),
            pltpu.VMEM((ctxs, 2, 8, HEAD), jnp.int32),
            pltpu.VMEM((HEAD, 2 * shard), jnp.bfloat16),
            pltpu.VMEM((2 * shard, 2 * HEAD), jnp.bfloat16),
            pltpu.VMEM((heads * rows, HEAD), jnp.float32),
            pltpu.VMEM((heads * rows, 2 * HEAD), jnp.float32),
            dma((6,)),
            dma((pools,)),
            dma((pools,)),
            dma((ctxs,)),
            dma((ctxs,)),
            dma((chips,)),
            dma((chips,)),
            dma((chips,)),
            dma((chips,)),
            dma((chips,)),
            dma((chips,)),
            dma((chips,)),
            dma((chips,)),
        ],
        compiler_params=pltpu.CompilerParams(
            collective_id=0, has_side_effects=True, vmem_limit_bytes=60 * 1024 * 1024
        ),
        name="attend_question",
    )(question_q, question_kv, cache_kv, placement, offsets, jnp.asarray(angle_tables(rows)))


def solution(mesh):
    counts = (mesh.shape["pool"], mesh.shape["ctx"])
    in_specs = (
        P("ctx", "pool"),
        P(None, "ctx", "pool"),
        P(("pool", "ctx"), None, None, None),
        P("ctx"),
        P("ctx"),
    )
    return jax.shard_map(
        functools.partial(shards, counts),
        mesh=mesh,
        in_specs=in_specs,
        out_specs=P("ctx", "pool"),
        check_vma=False,
    )
```

```python
import functools
import math

import jax
import jax.numpy as jnp
import numpy as np
from jax import lax
from jax.experimental import pallas as pl
from jax.experimental.pallas import tpu as pltpu
from jax.sharding import PartitionSpec as P

HEAD = 128
HALF = HEAD // 2
ROPE_BASE = 500000.0
MASKED = -1e30
LOG2_SCALE = HEAD**-0.5 * math.log2(math.e)
MESH = pl.DeviceIdType.MESH


def angle_tables(rows):
    frequency = ROPE_BASE ** (-np.arange(HALF, dtype=np.float64) / HALF)
    frequency = np.concatenate([frequency, frequency])
    angles = np.arange(rows)[:, None] * frequency[None, :]
    parts = [np.cos(angles), np.sin(angles), np.tile(frequency[None, :], (8, 1))]
    return np.concatenate(parts).astype(np.float32)


def flip_chip(chip, step, chips):
    result, bit = 0, 1
    while bit < chips:
        a = (chip // bit) % 2
        b = (step // bit) % 2
        result = result + bit * (a + b - 2 * a * b)
        bit *= 2
    return result


def signed(sine):
    lane = lax.broadcasted_iota(jnp.int32, sine.shape, 1)
    return jnp.where(lane < HALF, -sine, sine)


def turn(vectors, cosine, sine_signed):
    return vectors * cosine + pltpu.roll(vectors, HALF, 1) * sine_signed


def kernel(
    counts,
    q_hbm,
    kv_hbm,
    cache_hbm,
    place_hbm,
    offset_hbm,
    table_hbm,
    out_ref,
    place_ref,
    offset_ref,
    table_ref,
    q_raw,
    q_rot,
    kv_raw,
    own,
    pas,
    held,
    meta,
    k_now,
    v_now,
    top,
    acc,
    local_sem,
    pool_send,
    pool_recv,
    meta_send,
    meta_recv,
    own_send,
    own_recv,
    own_fwd_send,
    own_fwd_recv,
    pas_send,
    pas_recv,
    pas_fwd_send,
    pas_fwd_recv,
):
    pools, ctxs = counts
    chips = ctxs // 2
    p = lax.axis_index("pool")
    c = lax.axis_index("ctx")
    t = c // 2
    core = c % 2
    sibling = 2 * t + 1 - core
    rows = q_raw.shape[0]
    heads = q_rot.shape[0]
    hold = held.shape[1]
    block = held.shape[3]
    slots = place_ref.shape[0]
    shard = slots * block
    question_start = ctxs * slots * block

    load_q = pltpu.make_async_copy(q_hbm, q_raw, local_sem.at[0])
    load_kv = pltpu.make_async_copy(kv_hbm, kv_raw, local_sem.at[1])
    load_held = pltpu.make_async_copy(
        cache_hbm.at[:, :, :, pl.ds(pl.multiple_of(p * HEAD, HEAD), HEAD)],
        held.at[p],
        local_sem.at[2],
    )
    load_table = pltpu.make_async_copy(table_hbm, table_ref, local_sem.at[3])
    load_place = pltpu.make_async_copy(place_hbm, place_ref, local_sem.at[4])
    load_offset = pltpu.make_async_copy(offset_hbm, offset_ref, local_sem.at[5])
    load_place.start()
    load_offset.start()
    load_kv.start()
    load_table.start()
    load_held.start()
    load_q.start()

    barrier = pltpu.get_barrier_semaphore()
    for d in range(1, pools):
        pl.semaphore_signal(barrier, inc=1, device_id=((p + d) % pools, c), device_id_type=MESH)

    def greet(d, _):
        pl.semaphore_signal(barrier, inc=1, device_id=(p, (c + d) % ctxs), device_id_type=MESH)
        return 0

    lax.fori_loop(1, ctxs, greet, 0)

    load_place.wait()
    load_offset.wait()
    row8 = lax.broadcasted_iota(jnp.int32, (8, HEAD), 0)
    place_tile = jnp.full((8, HEAD), -1, jnp.int32)
    offset_tile = jnp.zeros((8, HEAD), jnp.int32)
    for i in range(slots):
        place_tile = jnp.where(row8 == i, place_ref[i], place_tile)
        offset_tile = jnp.where(row8 == i, offset_ref[i], offset_tile)
    meta[c, 0] = place_tile
    meta[c, 1] = offset_tile

    load_table.wait()
    freq = table_ref[2 * rows : 2 * rows + 8, :]
    base = (question_start + c * rows).astype(jnp.float32) * freq
    cos_base = jnp.cos(base)[0:1]
    sin_base = jnp.sin(base)[0:1]
    cos_row = table_ref[:rows]
    sin_row = table_ref[rows : 2 * rows]
    cos_q = cos_row * cos_base - sin_row * sin_base
    sin_q = signed(sin_row * cos_base + cos_row * sin_base)

    pl.semaphore_wait(barrier, pools - 1 + ctxs - 1)

    def pool_copy(d):
        target = (p + d) % pools
        return pltpu.make_async_remote_copy(
            src_ref=cache_hbm.at[:, :, :, pl.ds(pl.multiple_of(target * HEAD, HEAD), HEAD)],
            dst_ref=held.at[p],
            send_sem=pool_send.at[d],
            recv_sem=pool_recv.at[d],
            device_id=(target, c),
            device_id_type=MESH,
        )

    def meta_copy(d):
        return pltpu.make_async_remote_copy(
            src_ref=meta.at[c],
            dst_ref=meta.at[c],
            send_sem=meta_send.at[d],
            recv_sem=meta_recv.at[d],
            device_id=(p, (c + d) % ctxs),
            device_id_type=MESH,
        )

    def chip_copy(buffer, send, recv, d):
        return pltpu.make_async_remote_copy(
            src_ref=buffer.at[c],
            dst_ref=buffer.at[c],
            send_sem=send.at[d],
            recv_sem=recv.at[d],
            device_id=(p, 2 * flip_chip(t, d, chips) + core),
            device_id_type=MESH,
        )

    def forward_copy(buffer, send, recv, d):
        place = 2 * flip_chip(t, d, chips) + core
        return pltpu.make_async_remote_copy(
            src_ref=buffer.at[place],
            dst_ref=buffer.at[place],
            send_sem=send.at[d],
            recv_sem=recv.at[d],
            device_id=(p, sibling),
            device_id_type=MESH,
        )

    own_sems = (own, own_send, own_recv)
    own_fwd = (own, own_fwd_send, own_fwd_recv)
    pas_sems = (pas, pas_send, pas_recv)
    pas_fwd = (pas, pas_fwd_send, pas_fwd_recv)

    for d in range(1, pools):
        pool_copy(d).start()

    def start_meta(d, _):
        meta_copy(d).start()
        return 0

    lax.fori_loop(1, ctxs, start_meta, 0)

    load_kv.wait()
    turned = turn(kv_raw[0].astype(jnp.float32), cos_q, sin_q)
    for j in range(rows // HEAD):
        tile = turned[j * HEAD : (j + 1) * HEAD]
        own[c, 0, j * HEAD : (j + 1) * HEAD] = tile.T.astype(jnp.bfloat16)
    own[c, 1] = kv_raw[1]

    forward_copy(*own_fwd, 0).start()

    def start_own(d, _):
        @pl.when(flip_chip(t, d, chips) > t)
        def _():
            chip_copy(*own_sems, d).start()

        return 0

    lax.fori_loop(1, chips, start_own, 0)

    load_q.wait()
    for g in range(heads):
        vectors = q_raw[:, g * HEAD : (g + 1) * HEAD].astype(jnp.float32)
        q_rot[g] = turn(vectors, cos_q, sin_q).astype(jnp.bfloat16)

    ones = jnp.ones((2 * shard, HEAD), jnp.bfloat16)

    def attend(first):
        width = k_now.shape[1]
        wide = width // HEAD
        scores = jnp.dot(
            q_rot[...].reshape(heads * rows, HEAD), k_now[...], preferred_element_type=jnp.float32
        )
        if first:
            key = lax.broadcasted_iota(jnp.int32, (heads, rows, width), 2)
            query = lax.broadcasted_iota(jnp.int32, (heads, rows, width), 1) + core * rows
            scores = jnp.where((key <= query).reshape(scores.shape), scores, MASKED)
        peak = jnp.broadcast_to(jnp.max(scores, axis=1, keepdims=True), (heads * rows, HEAD))
        if not first:
            before = top[...]
            peak = jnp.maximum(before, peak)
        weights = jnp.exp2((scores - jnp.concatenate([peak] * wide, axis=1)) * LOG2_SCALE)
        product = jnp.dot(
            weights.astype(jnp.bfloat16), v_now[...], preferred_element_type=jnp.float32
        )
        if first:
            acc[...] = product
        else:
            shrink = jnp.exp2((before - peak) * LOG2_SCALE)
            acc[...] = acc[...] * jnp.concatenate([shrink, shrink], axis=1) + product
        top[...] = peak

    def gather_chunk(buffer, chip):
        for side in range(2):
            for j in range(shard // HEAD):
                at = side * shard + j * HEAD
                k_now[:, at : at + HEAD] = buffer[2 * chip + side, 0, j * HEAD : (j + 1) * HEAD]
        v_now[:, :HEAD] = buffer[pl.ds(2 * chip, 2), 1].reshape(2 * shard, HEAD)

    forward_copy(*own_fwd, 0).wait_recv()
    gather_chunk(own, t)
    v_now[:, HEAD:] = ones

    def own_arrive(d):
        @pl.when(flip_chip(t, d, chips) < t)
        def _():
            chip_copy(*own_sems, d).wait_recv()
            forward_copy(*own_fwd, d).start()

    def pas_arrive(d):
        chip_copy(*pas_sems, d).wait_recv()
        forward_copy(*pas_fwd, d).start()

    attend(True)
    own_arrive(1)

    def own_step(d, _):
        source = flip_chip(t, d, chips)

        def later():
            @pl.when(d + 1 < chips)
            def _():
                own_arrive(d + 1)

        @pl.when(source < t)
        def _():
            forward_copy(*own_fwd, d).wait_recv()
            gather_chunk(own, source)
            later()
            attend(False)

        @pl.when(source > t)
        def _():
            later()

        return 0

    def wait_meta(d, _):
        meta_copy(d).wait_recv()
        return 0

    lax.fori_loop(1, ctxs, wait_meta, 0)
    load_held.wait()
    for d in range(1, pools):
        pool_copy(d).wait_recv()

    places = meta[:, 0]
    offsets = meta[:, 1].astype(jnp.float32)
    live, where_to, rank = [], [], []
    filled = jnp.zeros((1, HEAD), jnp.float32)
    for b in range(pools * hold):
        block_id = ((b // hold) * ctxs + c) * hold + b % hold
        match = jnp.where(places == block_id, 1.0, 0.0)
        live.append(jnp.sum(jnp.sum(match, axis=0), axis=0, keepdims=True))
        where_to.append(jnp.sum(jnp.sum(match * offsets, axis=0), axis=0, keepdims=True))
        rank.append(filled)
        filled = filled + live[-1]
    turned_keys = []
    for k in range(slots):
        key_sum = jnp.zeros((block, HEAD), jnp.float32)
        value_sum = jnp.zeros((block, HEAD), jnp.float32)
        offset = jnp.zeros((1, HEAD), jnp.float32)
        for b in range(pools * hold):
            pick = jnp.where(rank[b] == float(k), live[b], 0.0)
            key_sum = key_sum + pick * held[b // hold, b % hold, 0].astype(jnp.float32)
            value_sum = value_sum + pick * held[b // hold, b % hold, 1].astype(jnp.float32)
            offset = offset + pick * where_to[b]
        angle = offset * freq
        cos_k = jnp.cos(angle)[0:1]
        sin_k = signed(jnp.sin(angle))[0:1]
        turned_keys.append(turn(key_sum, cos_k, sin_k))
        pas[c, 1, k * block : (k + 1) * block] = value_sum.astype(jnp.bfloat16)

    turned = jnp.concatenate(turned_keys, axis=0)
    for j in range(shard // HEAD):
        tile = turned[j * HEAD : (j + 1) * HEAD]
        pas[c, 0, j * HEAD : (j + 1) * HEAD] = tile.T.astype(jnp.bfloat16)

    forward_copy(*pas_fwd, 0).start()

    def start_pas(d, _):
        chip_copy(*pas_sems, d).start()
        return 0

    lax.fori_loop(1, chips, start_pas, 0)

    lax.fori_loop(1, chips, own_step, 0)

    hold_bits = hold.bit_length() - 1

    def pas_step(d, _):
        source = flip_chip(t, d, chips)

        forward_copy(*pas_fwd, d).wait_recv()
        v_now[:, :HEAD] = pas[pl.ds(2 * source, 2), 1].reshape(2 * shard, HEAD)
        seen = jnp.broadcast_to(own[c, 0, 0:HEAD, 0:1].astype(jnp.float32), (HEAD, HEAD))
        lane_slot = lax.broadcasted_iota(jnp.int32, (1, HEAD), 1) // block
        all_places = meta[:, 0]
        holder = lax.shift_right_logical(all_places, hold_bits) & (ctxs - 1)
        for side in range(2):
            column = 2 * source + side
            mine = jnp.where((all_places >= 0) & (holder == column), 1.0, 0.0)
            count = jnp.sum(jnp.sum(mine, axis=0), axis=0, keepdims=True)
            for k in range(slots):
                flag = jnp.broadcast_to(jnp.where(count > float(k), 1.0, 0.0), (block, HEAD))
                at = side * shard + k * block
                v_now[at : at + block, HEAD:] = flag.astype(jnp.bfloat16)

            for j in range(shard // HEAD):
                at = side * shard + j * HEAD
                slot = (lane_slot + j * (HEAD // block)).astype(jnp.float32)
                flag = jnp.broadcast_to(jnp.where(count > slot, 1.0, 0.0), (HEAD, HEAD))
                keys = pas[column, 0, j * HEAD : (j + 1) * HEAD].astype(jnp.float32)
                k_now[:, at : at + HEAD] = jnp.where(flag > 0.0, keys, seen).astype(jnp.bfloat16)

        def later():
            @pl.when(d + 1 < chips)
            def _():
                pas_arrive(d + 1)

        later()
        attend(False)
        return 0

    lax.fori_loop(0, chips, pas_step, 0)

    for g in range(heads):
        part = acc[g * rows : (g + 1) * rows]
        out_ref[:, g * HEAD : (g + 1) * HEAD] = (part[:, :HEAD] / part[:, HEAD:]).astype(
            jnp.bfloat16
        )

    for d in range(1, pools):
        pool_copy(d).wait_send()

    def end_meta(d, _):
        meta_copy(d).wait_send()
        return 0

    lax.fori_loop(1, ctxs, end_meta, 0)
    forward_copy(*own_fwd, 0).wait_send()
    forward_copy(*pas_fwd, 0).wait_send()

    def end_chips(d, _):
        other = flip_chip(t, d, chips)

        @pl.when(other > t)
        def _():
            chip_copy(*own_sems, d).wait_send()

        @pl.when(other < t)
        def _():
            forward_copy(*own_fwd, d).wait_send()

        chip_copy(*pas_sems, d).wait_send()
        forward_copy(*pas_fwd, d).wait_send()
        return 0

    lax.fori_loop(1, chips, end_chips, 0)


def shards(counts, question_q, question_kv, cache_kv, placement, offsets):
    pools, ctxs = counts
    chips = ctxs // 2
    rows, width = question_q.shape
    heads = width // HEAD
    hold, _, block, _ = cache_kv.shape
    slots = placement.shape[0]
    shard = slots * block
    dma = pltpu.SemaphoreType.DMA
    any_space = pl.BlockSpec(memory_space=pltpu.HBM)
    return pl.pallas_call(
        functools.partial(kernel, counts),
        out_shape=jax.ShapeDtypeStruct((rows, width), jnp.bfloat16),
        in_specs=[
            any_space,
            any_space,
            any_space,
            any_space,
            any_space,
            any_space,
        ],
        out_specs=pl.BlockSpec(memory_space=pltpu.VMEM),
        scratch_shapes=[
            pltpu.SMEM((slots,), jnp.int32),
            pltpu.SMEM((slots,), jnp.int32),
            pltpu.VMEM((2 * rows + 8, HEAD), jnp.float32),
            pltpu.VMEM((rows, width), jnp.bfloat16),
            pltpu.VMEM((heads, rows, HEAD), jnp.bfloat16),
            pltpu.VMEM((2, rows, HEAD), jnp.bfloat16),
            pltpu.VMEM((ctxs, 2, rows, HEAD), jnp.bfloat16),
            pltpu.VMEM((ctxs, 2, shard, HEAD), jnp.bfloat16),
            pltpu.VMEM((pools, hold, 2, block, HEAD), jnp.bfloat16),
            pltpu.VMEM((ctxs, 2, 8, HEAD), jnp.int32),
            pltpu.VMEM((HEAD, 2 * shard), jnp.bfloat16),
            pltpu.VMEM((2 * shard, 2 * HEAD), jnp.bfloat16),
            pltpu.VMEM((heads * rows, HEAD), jnp.float32),
            pltpu.VMEM((heads * rows, 2 * HEAD), jnp.float32),
            dma((6,)),
            dma((pools,)),
            dma((pools,)),
            dma((ctxs,)),
            dma((ctxs,)),
            dma((chips,)),
            dma((chips,)),
            dma((chips,)),
            dma((chips,)),
            dma((chips,)),
            dma((chips,)),
            dma((chips,)),
            dma((chips,)),
        ],
        compiler_params=pltpu.CompilerParams(
            collective_id=0, has_side_effects=True, vmem_limit_bytes=60 * 1024 * 1024
        ),
        name="attend_question",
    )(question_q, question_kv, cache_kv, placement, offsets, jnp.asarray(angle_tables(rows)))


def solution(mesh):
    counts = (mesh.shape["pool"], mesh.shape["ctx"])
    in_specs = (
        P("ctx", "pool"),
        P(None, "ctx", "pool"),
        P(("pool", "ctx"), None, None, None),
        P("ctx"),
        P("ctx"),
    )
    return jax.shard_map(
        functools.partial(shards, counts),
        mesh=mesh,
        in_specs=in_specs,
        out_specs=P("ctx", "pool"),
        check_vma=False,
    )
```
